1024 devices in a mesh: dp: 256 (over y_hi, z, x), head: 4 (over y_lo, core).
Axes of the slice: x: 4, y: 8 (y_hi: 4, y_lo: 2; y = y_hi * 2 + y_lo), z: 16, core: 2. Of those that a mesh axis runs over, the one named last changes fastest.
Arguments:
- q_cot: bfloat16 [65536, 6144], P('dp', 'head'), may hold values from -6 to 6
- k_cot: bfloat16 [65536, 4096], P('dp', 'head'), may hold values from -6 to 6
- q_latent: bfloat16 [65536, 1536], P('dp'), may hold values from -240 to 240
- q_gain: float32 [1536], replicated, may hold values from 0.1 to 1.9
- w_uq: bfloat16 [1536, 6144], P('dp', 'head'), may hold values from -0.15625 to 0.15625
- w_uk: bfloat16 [512, 4096], P('dp', 'head'), may hold values from -0.25 to 0.25
Outputs:
- d_query: bfloat16 [65536, 1536], P('dp', 'head')
- d_latent: bfloat16 [65536, 512], P('dp', 'head')
The draws below stay inside these ranges and needn't reach their ends.
All inputs are finite; a program needn't handle non-finite values.
Results may differ from the reference program's by a relative error of at most 0.0012.
Values may be sent and summed in bfloat16 or wider, within the bound.
A program may use at most 32 MiB of HBM per device.

```python
import math
import jax
import jax.numpy as jnp
from jax import lax

QR = 1536
KVR = 512
NOPE = 128
TOK_DEV = 256
QH = 192
HEADS = 32
TOKENS = 65536


def draw_q_latent(key, part):
    key = jax.random.fold_in(key, 7)
    key_base = jax.random.fold_in(key, 1)
    key_rowscale = jax.random.fold_in(key, 2)
    key_colscale = jax.random.fold_in(key, 3)
    base_draw = jnp.clip(jax.random.normal(key_base, (TOKENS, QR), jnp.float32), -6.0, 6.0)
    row_scale = jnp.exp(jax.random.uniform(key_rowscale, (TOKENS, 1), jnp.float32, 0.0, math.log(10.0)))
    col_scale = jnp.exp(jax.random.uniform(key_colscale, (1, QR), jnp.float32, math.log(0.2), math.log(4.0)))
    return (base_draw * row_scale * col_scale).astype(jnp.bfloat16)


def level_of(rng, shape, cuts, smallest, high):
    def one(axis_at, parts):
        draws = jax.random.uniform(jax.random.fold_in(jax.random.fold_in(rng, 6), axis_at), (parts,), jnp.float32, smallest / len(cuts), high / len(cuts))
        return jnp.repeat(jnp.exp(draws), shape[axis_at] // parts).reshape((-1,) + (1,) * (len(shape) - axis_at - 1))

    level = one(*cuts[0])
    for cut in cuts[1:]:
        level = level * one(*cut)
    return level


def gaussian(stream_key, shape, width, limit, pieces=(), held_as=jnp.bfloat16):
    factor_of = level_of(stream_key, shape, pieces, -0.22, 0.18) if pieces else 1.0
    result = jax.random.normal(stream_key, shape, jnp.float32) * width * factor_of
    return jnp.minimum(jnp.maximum(result, -limit), limit).astype(held_as)


def setup_inputs(seed: int = 0) -> dict:
    key_of = jax.random.split(jax.random.key(seed), 7)
    return {
        "q_cot": gaussian(key_of[0], (TOKENS, HEADS * QH), 1.0, 6.0, ((0, 256), (1, 4))),
        "k_cot": gaussian(key_of[1], (TOKENS, HEADS * NOPE), 1.0, 6.0, ((0, 256), (1, 4))),
        "q_latent": draw_q_latent(jax.random.fold_in(key_of[6], 71), 0),
        "q_gain": jnp.clip(1.0 + 0.18 * jax.random.normal(key_of[3], (QR,), jnp.float32), 0.1, 1.9),
        "w_uq": gaussian(key_of[4], (QR, HEADS * QH), QR ** -0.5, 0.15625, ((0, 256), (1, 4))),
        "w_uk": gaussian(key_of[5], (KVR, HEADS * NOPE), KVR ** -0.5, 0.25, ((0, 256), (1, 4))),
    }


norm_eps = 1e-06

def reference(q_cot, k_cot, q_latent, q_gain, w_uq, w_uk):
    blocks = TOKENS // TOK_DEV

    def one_block(inputs):
        query_cot, key_cot, latent_in = inputs
        d_normed = jnp.dot(query_cot, w_uq.T, preferred_element_type=jnp.float32)
        d_latent = jnp.dot(key_cot, w_uk.T, preferred_element_type=jnp.float32).astype(jnp.bfloat16)
        latent_float = latent_in.astype(jnp.float32)
        root_mean = jnp.sqrt(lax.optimization_barrier(jnp.mean(latent_float * latent_float, axis=1, keepdims=True)) + norm_eps)
        normed = latent_float / root_mean
        scaled = q_gain[None, :] * d_normed
        row_dot = lax.optimization_barrier(jnp.mean(scaled * normed, axis=1, keepdims=True))
        d_query = ((scaled - normed * row_dot) / root_mean).astype(jnp.bfloat16)
        return (d_query, d_latent)
    query_all, latent_all = lax.map(one_block, (q_cot.reshape(blocks, TOK_DEV, q_cot.shape[1]), k_cot.reshape(blocks, TOK_DEV, k_cot.shape[1]), q_latent.reshape(blocks, TOK_DEV, q_latent.shape[1])))
    return (query_all.reshape(TOKENS, QR), latent_all.reshape(TOKENS, KVR))
```

```python
import jax
import jax.numpy as jnp
from jax import lax
from jax.experimental import pallas as pl
from jax.experimental.pallas import tpu as pltpu
from jax.sharding import PartitionSpec as P

norm_eps = 1e-06
MESH = pl.DeviceIdType.MESH

NX, NZ, NYH = 4, 16, 4
TOK, QR, KVR = 256, 1536, 512
QF, KF = 1536, 1024
WIDE = 2 * QF
C1 = 1024
C2 = WIDE - C1
J1 = 2
P1 = C1 // J1
HALF = C2 // 2
SHARE = QR // 4
LSHARE = KVR // 4


def kernel(
    q_cot, k_cot, q_lat_hbm, gain, w_uq, w_uk, d_query, d_latent,
    a_all, w1, w2, y_land, y_send, stage, q_lat, root, gain_normed, products,
    part, part_in, dot_mine, dot_in,
    local_sem, a_send, a_recv, y_ssem, y_rsem, x1_send, x1_recv,
    z1_send, z1_recv, z2_send, z2_recv, x2_send, x2_first, x2_rest, fwd_send,
    part_send, part_recv, dot_send, dot_recv,
):
    dp, head = lax.axis_index("dp"), lax.axis_index("head")
    x, z, yh = dp % NX, (dp // NX) % NZ, dp // (NX * NZ)
    ylo, core = head // 2, head % 2

    def at(nyh, nz, nx, nylo, ncore):
        return ((nyh * NZ + nz) * NX + nx, nylo * 2 + ncore)

    xr, xl, xo = (x + 1) % NX, (x + NX - 1) % NX, (x + 2) % NX
    zr, zl = (z + 1) % NZ, (z + NZ - 1) % NZ
    sibling = at(yh, z, x, ylo, 1 - core)
    facing = at(yh, z, x, 1 - ylo, core)
    facing_sibling = at(yh, z, x, 1 - ylo, 1 - core)
    to_x = (at(yh, z, xr, ylo, core), at(yh, z, xl, ylo, core))
    to_x_over = at(yh, z, xo, ylo, core)
    to_z = (at(yh, zr, x, ylo, core), at(yh, zl, x, ylo, core))

    def remote(src, dst, ssem, rsem, device):
        return pltpu.make_async_remote_copy(
            src_ref=src, dst_ref=dst, send_sem=ssem, recv_sem=rsem,
            device_id=device, device_id_type=MESH,
        )

    own_q = pltpu.make_async_copy(q_cot, a_all.at[core, pl.ds(0, TOK)], local_sem.at[0])
    own_k = [
        pltpu.make_async_copy(
            k_cot.at[:, pl.ds(h * 512, 512)],
            a_all.at[core, pl.ds(TOK, TOK), pl.ds(h * 768, 512)],
            local_sem.at[1 + h],
        )
        for h in range(2)
    ]
    own_lat = pltpu.make_async_copy(q_lat_hbm, q_lat, local_sem.at[3])
    own_lat.start()
    own_q.start()
    for copy in own_k:
        copy.start()

    barrier = pltpu.get_barrier_semaphore()
    partners = [to_x[0], to_x[1], to_x_over, to_z[0], to_z[1], facing, facing_sibling, sibling]
    for j in range(1, NYH):
        for c in range(2):
            partners.append(at((yh + j) % NYH, z, x, ylo, c))
    for device in partners:
        pl.semaphore_signal(barrier, inc=1, device_id=device, device_id_type=MESH)

    uq = w_uq[...].astype(jnp.float32)
    uk = w_uk[...].astype(jnp.float32)
    for h in range(2):
        stage[8 * h : 8 * h + 6, 0:768] = uq[:, h * 768 : (h + 1) * 768]
        stage[8 * h + 6 : 8 * h + 8, 0:512] = uk[:, h * 512 : (h + 1) * 512]
        stage[8 * h + 6 : 8 * h + 8, 512:768] = jnp.zeros((2, 256), jnp.float32)
    y_send[...] = stage[:, 0:768].astype(jnp.bfloat16)

    pl.semaphore_wait(barrier, len(partners))

    y_core, y_half = yh % 2, yh // 2
    for j in range(NYH):
        stays = jnp.logical_and(yh == j, y_core == core)

        @pl.when(jnp.logical_not(stays))
        def _(j=j):
            remote(
                y_send, y_land.at[y_half, core], y_ssem.at[j], y_rsem.at[y_half, core],
                at(j, z, x, ylo, y_core),
            ).start()

    mine = y_core == core

    @pl.when(mine)
    def _():
        y_land[y_half, core] = y_send[...]

    give_q = remote(
        q_cot, a_all.at[core, pl.ds(0, TOK)], a_send.at[0], a_recv.at[0], sibling
    )
    give_k = [
        remote(
            k_cot.at[:, pl.ds(h * 512, 512)],
            a_all.at[core, pl.ds(TOK, TOK), pl.ds(h * 768, 512)],
            a_send.at[1 + h], a_recv.at[1 + h], sibling,
        )
        for h in range(2)
    ]
    give_q.start()
    for copy in give_k:
        copy.start()

    for c in range(2):
        for h in range(2):
            a_all[c, TOK : 2 * TOK, h * 768 + 512 : (h + 1) * 768] = jnp.zeros((TOK, 256), jnp.bfloat16)

    for half in range(2):
        for c in range(2):
            source_yh = core + 2 * half
            local = jnp.logical_and(source_yh == yh, core == c)

            @pl.when(jnp.logical_not(local))
            def _(half=half, c=c, source_yh=source_yh):
                remote(
                    y_send, y_land.at[half, c], y_ssem.at[0], y_rsem.at[half, c],
                    at((yh + 1) % NYH, z, x, ylo, c),
                ).wait_recv()

            piece = y_land[half, c].astype(jnp.float32)
            for h in range(2):
                columns = slice(c * QF + h * 768, c * QF + (h + 1) * 768)
                stage[6 * half : 6 * half + 6, columns] = piece[8 * h : 8 * h + 6]
                stage[12 + 2 * half : 14 + 2 * half, columns] = piece[8 * h + 6 : 8 * h + 8]

    def rows_of(nx):
        return pl.ds(pl.multiple_of(nx * 16, 16), 16)

    w1[z, rows_of(x), :] = stage[:, 0:C1].astype(jnp.bfloat16)
    w2[z, rows_of(x), :] = stage[:, C1:WIDE].astype(jnp.bfloat16)

    def ring2(way, block):
        src = w2.at[block, rows_of(x)]
        return remote(src, src, z2_send.at[0], z2_recv.at[block], to_z[way])

    def cross(way, block, half, first):
        src = w2.at[block, rows_of(x), pl.ds(half * HALF, HALF)]
        sem = x2_first.at[way, block] if first else x2_rest.at[block]
        return remote(src, src, x2_send.at[0], sem, to_x[way])

    def start_cross(block):
        for way in range(2):
            cross(way, block, way, True).start()
        for way in range(2):
            cross(way, block, 1 - way, False).start()

    def ring1(way, block, j):
        src = w1.at[block, :, pl.ds(j * P1, P1)]
        return remote(src, src, z1_send.at[0], z1_recv.at[block, j], to_z[way])

    ring2(0, z).start()
    ring2(1, z).start()
    src1 = w1.at[z, rows_of(x)]
    for k, device in enumerate((to_x[0], to_x[1], to_x_over)):
        remote(src1, src1, x1_send.at[0], x1_recv.at[x], device).start()
    start_cross(z)

    own_lat.wait()
    latent = q_lat[...].astype(jnp.float32)
    root_mean = jnp.sqrt(jnp.mean(latent * latent, axis=1, keepdims=True) + norm_eps)
    root[...] = jnp.broadcast_to(root_mean, (TOK, 128))
    for half in range(2):
        columns = pl.ds(pl.multiple_of((core + 2 * half) * SHARE, 128), SHARE)
        normed = q_lat[:, columns].astype(jnp.float32) / root_mean
        gain_normed[half] = (gain[:, columns] * normed).T
    dot_mine[...] = jnp.zeros_like(dot_mine)

    for k in range(1, NX):
        nx = (x + k) % NX
        dst = w1.at[z, rows_of(nx)]
        remote(dst, dst, x1_send.at[0], x1_recv.at[nx], to_x_over).wait_recv()
    for j in range(J1):
        ring1(0, z, j).start()
        ring1(1, z, j).start()

    own_q.wait()
    give_q.wait_recv()
    for h in range(2):
        own_k[h].wait()
        give_k[h].wait_recv()

    def multiply(block_a, block_b):
        total = None
        for t in range(WIDE // 512):
            ref, start = (w1, t * 512) if t * 512 < C1 else (w2, t * 512 - C1)
            left = jnp.concatenate(
                [ref[block_a, :, start : start + 512], ref[block_b, :, start : start + 512]], axis=0
            )
            c, a_start = t * 512 // QF, t * 512 % QF
            term = lax.dot_general(
                left, a_all[c, :, a_start : a_start + 512], (((1,), (1,)), ((), ())),
                preferred_element_type=jnp.float32,
            )
            total = term if total is None else total + term
        products[...] = total
        dot = dot_mine[...]
        for g, block in enumerate((block_a, block_b)):
            for half in range(2):
                for nx in range(NX):
                    base = g * 64 + nx * 16
                    part[half, block, 6 * nx : 6 * nx + 6, :] = products[
                        base + 6 * half : base + 6 * half + 6, 0:TOK
                    ]
                    part[half, block, 24 + 2 * nx : 26 + 2 * nx, :] = products[
                        base + 12 + 2 * half : base + 14 + 2 * half, TOK : 2 * TOK
                    ]
            send_part(block).start()
            for half in range(2):
                weighted = (
                    part[half, block, 0:24, :]
                    * gain_normed[half, pl.ds(pl.multiple_of(block * 24, 8), 24), :]
                )
                dot = dot + (weighted[0:8] + weighted[8:16] + weighted[16:24])
        dot_mine[...] = dot

    def send_part(block):
        return remote(
            part.at[1 - ylo, block], part_in.at[block], part_send.at[0], part_recv.at[block], facing
        )

    def step(s, carry):
        behind, ahead = (z - s + NZ) % NZ, (z + s) % NZ
        both = jnp.logical_and(s >= 1, s <= 7)

        @pl.when(jnp.logical_and(s >= 1, s <= 8))
        def _():
            ring2(0, behind).wait_recv()

            @pl.when(s < 8)
            def _():
                ring2(0, behind).start()

            @pl.when(s < 8)
            def _():
                ring2(1, ahead).wait_recv()

            @pl.when(s < 7)
            def _():
                ring2(1, ahead).start()

            start_cross(behind)

            @pl.when(s < 8)
            def _():
                start_cross(ahead)

            for j in range(J1):
                ring1(0, behind, j).wait_recv()

                @pl.when(s < 8)
                def _(j=j):
                    ring1(0, behind, j).start()

                @pl.when(s < 8)
                def _(j=j):
                    ring1(1, ahead, j).wait_recv()

                @pl.when(s < 7)
                def _(j=j):
                    ring1(1, ahead, j).start()

        def forward(block):
            for way, nx in ((0, xl), (1, xr)):
                src = w2.at[block, rows_of(nx), pl.ds(way * HALF, HALF)]
                remote(src, src, fwd_send.at[0], x2_first.at[way, block], to_x[way]).wait_recv()
                remote(src, src, fwd_send.at[0], x2_rest.at[block], to_x[way]).start()

        before, after = (z - s + 1 + NZ) % NZ, (z + s - 1) % NZ

        @pl.when(jnp.logical_and(s >= 1, s <= 9))
        def _():
            forward(before)

        @pl.when(jnp.logical_and(s >= 2, s <= 8))
        def _():
            forward(after)

        @pl.when(s >= 3)
        def _():
            p = s - 2
            block_a = (z - p + NZ) % NZ
            block_b = jnp.where(p == 8, z, (z + p) % NZ)
            for block in (block_a, block_b):
                dst = w2.at[block, :, pl.ds(0, HALF)]
                remote(dst, dst, x2_send.at[0], x2_rest.at[block], to_x[0]).wait_recv()
            multiply(block_a, block_b)

        return carry

    lax.fori_loop(1, 11, step, 0)

    dot_in[head] = dot_mine[...]
    for device in (facing, facing_sibling, sibling):
        remote(dot_mine, dot_in.at[head], dot_send.at[0], dot_recv.at[head], device).start()

    for j in range(NYH):
        stays = jnp.logical_and(yh == j, y_core == core)

        @pl.when(jnp.logical_not(stays))
        def _(j=j):
            remote(
                y_send, y_land.at[y_half, core], y_ssem.at[j], y_rsem.at[y_half, core],
                at(j, z, x, ylo, y_core),
            ).wait_send()

    give_q.wait_send()
    for copy in give_k:
        copy.wait_send()

    def sent(ref, sem):
        remote(ref, ref, sem.at[0], dot_recv.at[0], facing).wait_send()

    sent(w1.at[0, pl.ds(0, 48)], x1_send)
    sent(w1.at[pl.ds(0, NZ - 1)], z1_send)
    sent(w2.at[pl.ds(0, NZ - 1), pl.ds(0, 16)], z2_send)
    sent(w2.at[:, pl.ds(0, 32)], x2_send)
    sent(w2.at[:, pl.ds(0, 16)], fwd_send)

    for k in range(1, 4):
        other = (head + k) % 4
        remote(dot_mine, dot_in.at[other], dot_send.at[0], dot_recv.at[other], sibling).wait_recv()
    dots = dot_in[0] + dot_in[1] + dot_in[2] + dot_in[3]
    row_dot = jnp.sum(dots, axis=0, keepdims=True) / QR
    row_dot = jnp.broadcast_to(row_dot, (128, TOK)).T[:, 0:1]

    def arrived(block, carry):
        remote(
            part_in.at[block], part_in.at[block], part_send.at[0], part_recv.at[block], facing
        ).wait_recv()
        return carry

    lax.fori_loop(0, NZ, arrived, 0)
    whole = part[ylo] + part_in[...]
    d_normed = whole[:, 0:24, :].reshape(SHARE, TOK).T
    d_latent[...] = whole[:, 24:32, :].reshape(LSHARE, TOK).T.astype(jnp.bfloat16)
    columns = pl.ds(pl.multiple_of(head * SHARE, 128), SHARE)
    root_mean = root[:, 0:1]
    normed = q_lat[:, columns].astype(jnp.float32) / root_mean
    scaled = gain[:, columns] * d_normed
    d_query[...] = ((scaled - normed * row_dot) / root_mean).astype(jnp.bfloat16)
    sent(part_in, part_send)
    sent(dot_in.at[pl.ds(0, 3)], dot_send)


def on_device(q_cot, k_cot, q_latent, q_gain, w_uq, w_uk):
    vmem = pl.BlockSpec(memory_space=pltpu.VMEM)
    hbm = pl.BlockSpec(memory_space=pl.ANY)
    f32, bf16 = jnp.float32, jnp.bfloat16
    dma = pltpu.SemaphoreType.DMA
    return pl.pallas_call(
        kernel,
        out_shape=(
            jax.ShapeDtypeStruct((TOK, SHARE), bf16),
            jax.ShapeDtypeStruct((TOK, LSHARE), bf16),
        ),
        in_specs=[hbm, hbm, hbm, vmem, vmem, vmem],
        out_specs=(vmem, vmem),
        scratch_shapes=[
            pltpu.VMEM((2, 2 * TOK, QF), bf16),
            pltpu.VMEM((NZ, 64, C1), bf16),
            pltpu.VMEM((NZ, 64, C2), bf16),
            pltpu.VMEM((2, 2, 16, 768), bf16),
            pltpu.VMEM((16, 768), bf16),
            pltpu.VMEM((16, WIDE), f32),
            pltpu.VMEM((TOK, QR), bf16),
            pltpu.VMEM((TOK, 128), f32),
            pltpu.VMEM((2, SHARE, TOK), f32),
            pltpu.VMEM((128, 2 * TOK), f32),
            pltpu.VMEM((2, NZ, 32, TOK), f32),
            pltpu.VMEM((NZ, 32, TOK), f32),
            pltpu.VMEM((8, TOK), f32),
            pltpu.VMEM((4, 8, TOK), f32),
            dma((4,)),
            dma((3,)),
            dma((3,)),
            dma((4,)),
            dma((2, 2)),
            dma((1,)),
            dma((NX,)),
            dma((1,)),
            dma((NZ, J1)),
            dma((1,)),
            dma((NZ,)),
            dma((1,)),
            dma((2, NZ)),
            dma((NZ,)),
            dma((1,)),
            dma((1,)),
            dma((NZ,)),
            dma((1,)),
            dma((4,)),
        ],
        compiler_params=pltpu.CompilerParams(
            collective_id=0, has_side_effects=True, vmem_limit_bytes=40 * 2**20
        ),
        name="latent_backward",
    )(q_cot, k_cot, q_latent, q_gain.reshape(1, QR), w_uq, w_uk)


def solution(mesh):
    return jax.shard_map(
        on_device,
        mesh=mesh,
        in_specs=(
            P("dp", "head"),
            P("dp", "head"),
            P("dp", None),
            P(),
            P("dp", "head"),
            P("dp", "head"),
        ),
        out_specs=(P("dp", "head"), P("dp", "head")),
        check_vma=False,
    )
```

```python
import jax
import jax.numpy as jnp
from jax import lax
from jax.experimental import pallas as pl
from jax.experimental.pallas import tpu as pltpu
from jax.sharding import PartitionSpec as P

norm_eps = 1e-06
MESH = pl.DeviceIdType.MESH

NX, NZ, NYH = 4, 16, 4
TOK, QR, KVR = 256, 1536, 512
QF, KF = 1536, 1024
C1 = 1024
C2 = 1792
HALF = C2 // 2
SHARE = QR // 4
LSHARE = KVR // 4


def kernel(
    q_cot, k_cot, q_lat_hbm, gain_flat, w_uq, w_uk, d_query, d_latent,
    a1, a2, w1, w2, y_land, y_send, stage1, stage2, q_lat, root, gain_normed, products,
    part, part_in, dot_mine, dot_in, gain,
    local_sem, a_send, a_recv, y_ssem, y_rsem, x1_send, x1_recv,
    z1_send, z1_recv, z2_send, z2_recv, x2_send, x2_first, x2_rest, fwd_send,
    part_send, part_recv, dot_send, dot_recv,
):
    dp, head = lax.axis_index("dp"), lax.axis_index("head")
    x, z, yh = dp % NX, (dp // NX) % NZ, dp // (NX * NZ)
    ylo, core = head // 2, head % 2

    def at(nyh, nz, nx, nylo, ncore):
        return ((nyh * NZ + nz) * NX + nx, nylo * 2 + ncore)

    xr, xl, xo = (x + 1) % NX, (x + NX - 1) % NX, (x + 2) % NX
    zr, zl = (z + 1) % NZ, (z + NZ - 1) % NZ
    sibling = at(yh, z, x, ylo, 1 - core)
    facing = at(yh, z, x, 1 - ylo, core)
    facing_sibling = at(yh, z, x, 1 - ylo, 1 - core)
    to_x = (at(yh, z, xr, ylo, core), at(yh, z, xl, ylo, core))
    to_x_over = at(yh, z, xo, ylo, core)
    to_z = (at(yh, zr, x, ylo, core), at(yh, zl, x, ylo, core))

    def remote(src, dst, ssem, rsem, device):
        return pltpu.make_async_remote_copy(
            src_ref=src, dst_ref=dst, send_sem=ssem, recv_sem=rsem,
            device_id=device, device_id_type=MESH,
        )

    def cotangents():
        for h in range(2):
            yield q_cot.at[:, pl.ds(h * 768, 512)], a2.at[core, h, pl.ds(0, TOK)]
            yield q_cot.at[:, pl.ds(h * 768 + 512, 256)], a1.at[core, h]
            yield k_cot.at[:, pl.ds(h * 512, 512)], a2.at[core, h, pl.ds(TOK, TOK)]

    own_lat = pltpu.make_async_copy(q_lat_hbm, q_lat, local_sem.at[6])
    own_lat.start()
    own_rows = [
        pltpu.make_async_copy(src, dst, local_sem.at[i])
        for i, (src, dst) in enumerate(cotangents())
    ]
    for copy in own_rows:
        copy.start()

    barrier = pltpu.get_barrier_semaphore()
    partners = [to_x[0], to_x[1], to_x_over, to_z[0], to_z[1], facing, facing_sibling, sibling]
    for j in range(1, NYH):
        for c in range(2):
            partners.append(at((yh + j) % NYH, z, x, ylo, c))
    for device in partners:
        pl.semaphore_signal(barrier, inc=1, device_id=device, device_id_type=MESH)

    uq = w_uq[...].astype(jnp.float32)
    uk = w_uk[...].astype(jnp.float32)
    for h in range(2):
        stage1[8 * h : 8 * h + 6] = uq[:, h * 768 : (h + 1) * 768]
        stage1[8 * h + 6 : 8 * h + 8, 0:512] = uk[:, h * 512 : (h + 1) * 512]
        stage1[8 * h + 6 : 8 * h + 8, 512:768] = jnp.zeros((2, 256), jnp.float32)
    y_send[...] = stage1[...].astype(jnp.bfloat16)

    pl.semaphore_wait(barrier, len(partners))

    y_core, y_half = yh % 2, yh // 2
    for j in range(NYH):
        stays = jnp.logical_and(yh == j, y_core == core)

        @pl.when(jnp.logical_not(stays))
        def _(j=j):
            remote(
                y_send, y_land.at[y_half, core], y_ssem.at[j], y_rsem.at[y_half, core],
                at(j, z, x, ylo, y_core),
            ).start()

    mine = y_core == core

    @pl.when(mine)
    def _():
        y_land[y_half, core] = y_send[...]

    give = [
        remote(src, dst, a_send.at[i], a_recv.at[i], sibling)
        for i, (src, dst) in enumerate(cotangents())
    ]
    for copy in give:
        copy.start()

    gain[...] = gain_flat[...].reshape(1, QR)
    own_lat.wait()
    latent = q_lat[...].astype(jnp.float32)
    root_mean = jnp.sqrt(jnp.mean(latent * latent, axis=1, keepdims=True) + norm_eps)
    root[...] = jnp.broadcast_to(root_mean, (TOK, 128))
    for half in range(2):
        columns = pl.ds(pl.multiple_of((core + 2 * half) * SHARE, 128), SHARE)
        normed = q_lat[:, columns].astype(jnp.float32) / root_mean
        gain_normed[half] = (gain[:, columns] * normed).T
    dot_mine[...] = jnp.zeros_like(dot_mine)

    for half in range(2):
        for c in range(2):
            source_yh = core + 2 * half
            local = jnp.logical_and(source_yh == yh, core == c)

            @pl.when(jnp.logical_not(local))
            def _(half=half, c=c, source_yh=source_yh):
                remote(
                    y_send, y_land.at[half, c], y_ssem.at[0], y_rsem.at[half, c],
                    at((yh + 1) % NYH, z, x, ylo, c),
                ).wait_recv()

            piece = y_land[half, c].astype(jnp.float32)
            for h in range(2):
                rank, latents, group = piece[8 * h : 8 * h + 6], piece[8 * h + 6 : 8 * h + 8], 2 * c + h
                stage2[6 * half : 6 * half + 6, group * 512 : group * 512 + 512] = rank[:, 0:512]
                stage2[12 + 2 * half : 14 + 2 * half, group * 512 : group * 512 + 512] = latents[:, 0:512]
                if group < 3:
                    stage1[6 * half : 6 * half + 6, group * 256 : group * 256 + 256] = rank[:, 512:768]
                elif half == 0:
                    stage1[12:16, 0:256] = rank[0:4, 512:768]
                    stage1[12:14, 256:512] = rank[4:6, 512:768]
                else:
                    stage1[14:16, 256:512] = rank[0:2, 512:768]
                    stage1[12:16, 512:768] = rank[2:6, 512:768]

    def rows_of(nx):
        return pl.ds(pl.multiple_of(nx * 16, 16), 16)

    w1[z, rows_of(x), 0:768] = stage1[...].astype(jnp.bfloat16)
    w1[z, rows_of(x), 768:C1] = stage2[:, C2:2048].astype(jnp.bfloat16)
    w2[z, rows_of(x), :] = stage2[:, 0:C2].astype(jnp.bfloat16)

    def ring2(way, block):
        src = w2.at[block, rows_of(x)]
        return remote(src, src, z2_send.at[0], z2_recv.at[block], to_z[way])

    def cross(way, block, half, first):
        src = w2.at[block, rows_of(x), pl.ds(half * HALF, HALF)]
        sem = x2_first.at[way, block] if first else x2_rest.at[block]
        return remote(src, src, x2_send.at[0], sem, to_x[way])

    def start_cross(block):
        for way in range(2):
            cross(way, block, way, True).start()
        for way in range(2):
            cross(way, block, 1 - way, False).start()

    def ring1(way, block, nx):
        src = w1.at[block, rows_of(nx)]
        return remote(src, src, z1_send.at[0], z1_recv.at[block, nx], to_z[way])

    ring2(0, z).start()
    ring2(1, z).start()
    src1 = w1.at[z, rows_of(x)]
    for k, device in enumerate((to_x[0], to_x[1], to_x_over)):
        remote(src1, src1, x1_send.at[0], x1_recv.at[x], device).start()
    ring1(0, z, x).start()
    ring1(1, z, x).start()
    start_cross(z)

    for nx in (xr, xl, xo):
        dst = w1.at[z, rows_of(nx)]
        remote(dst, dst, x1_send.at[0], x1_recv.at[nx], to_x_over).wait_recv()
        ring1(0, z, nx).start()
        ring1(1, z, nx).start()

    for i in range(6):
        own_rows[i].wait()
        give[i].wait_recv()

    def multiply(block_a, block_b):
        def both(ref, start, size):
            return jnp.concatenate(
                [ref[block_a, :, start : start + size], ref[block_b, :, start : start + size]], axis=0
            )

        def times(left, right):
            return lax.dot_general(
                left, right, (((1,), (1,)), ((), ())), preferred_element_type=jnp.float32
            )

        total = times(both(w2, 0, 512), a2[0, 0])
        for t in range(1, 3):
            total = total + times(both(w2, t * 512, 512), a2[t // 2, t % 2])
        last = jnp.concatenate([both(w2, 1536, 256), both(w1, 768, 256)], axis=1)
        total = total + times(last, a2[1, 1])
        products[:, 0 : 2 * TOK] = total
        firsts = [both(w1, t * 256, 256) for t in range(3)]
        total = times(firsts[0], a1[0, 0]) + times(firsts[1], a1[0, 1]) + times(firsts[2], a1[1, 0])
        products[:, 0:TOK] += total
        for t in range(3):
            products[:, (2 + t) * TOK : (3 + t) * TOK] = times(firsts[t], a1[1, 1])
        for base in range(0, 128, 16):
            for t in range(3):
                products[base + 4 * t : base + 4 * t + 4, 0:TOK] += products[
                    base + 12 : base + 16, (2 + t) * TOK : (3 + t) * TOK
                ]
        dot = dot_mine[...]
        for g, block in enumerate((block_a, block_b)):
            for half in range(2):
                for nx in range(NX):
                    base = g * 64 + nx * 16
                    part[half, block, 6 * nx : 6 * nx + 6, :] = products[
                        base + 6 * half : base + 6 * half + 6, 0:TOK
                    ]
                    part[half, block, 24 + 2 * nx : 26 + 2 * nx, :] = products[
                        base + 12 + 2 * half : base + 14 + 2 * half, TOK : 2 * TOK
                    ]
            send_part(block).start()
            for half in range(2):
                weighted = (
                    part[half, block, 0:24, :]
                    * gain_normed[half, pl.ds(pl.multiple_of(block * 24, 8), 24), :]
                )
                dot = dot + (weighted[0:8] + weighted[8:16] + weighted[16:24])
        dot_mine[...] = dot

    def send_part(block):
        return remote(
            part.at[1 - ylo, block], part_in.at[block], part_send.at[0], part_recv.at[block], facing
        )

    def cross_pair(d):
        start_cross((z - d + NZ) % NZ)

        @pl.when(d < 8)
        def _():
            start_cross((z + d) % NZ)

    def forward(block):
        for way, nx in ((0, xl), (1, xr)):
            src = w2.at[block, rows_of(nx), pl.ds(way * HALF, HALF)]
            remote(src, src, fwd_send.at[0], x2_first.at[way, block], to_x[way]).wait_recv()
            remote(src, src, fwd_send.at[0], x2_rest.at[block], to_x[way]).start()

    def ring1_unit(unit):
        step_at, k = unit // 4 + 1, unit % 4
        nx = jnp.where(k == 0, x, jnp.where(k == 1, xr, jnp.where(k == 2, xl, xo)))
        behind, ahead = (z - step_at + NZ) % NZ, (z + step_at) % NZ
        ring1(0, behind, nx).wait_recv()

        @pl.when(step_at < 8)
        def _():
            ring1(0, behind, nx).start()
            ring1(1, ahead, nx).wait_recv()

        @pl.when(step_at < 7)
        def _():
            ring1(1, ahead, nx).start()

    def step(i, carry):
        behind, ahead = (z - i + NZ) % NZ, (z + i) % NZ

        @pl.when(i <= 8)
        def _():
            ring2(0, behind).wait_recv()

            @pl.when(i < 8)
            def _():
                ring2(0, behind).start()
                ring2(1, ahead).wait_recv()

            @pl.when(i < 7)
            def _():
                ring2(1, ahead).start()

            cross_pair(i)
            for k in range(3):
                ring1_unit(3 * i - 3 + k)

        @pl.when(i >= 9)
        def _():
            for k in range(4):
                ring1_unit(4 * i - 12 + k)

        @pl.when(i <= 9)
        def _():
            forward((z - i + 1 + NZ) % NZ)

        @pl.when(jnp.logical_and(i >= 2, i <= 8))
        def _():
            forward((z + i - 1) % NZ)

        @pl.when(i >= 3)
        def _():
            d = i - 2
            block_a = (z - d + NZ) % NZ
            block_b = jnp.where(d == 8, z, (z + d) % NZ)
            for block in (block_a, block_b):
                dst = w2.at[block, :, pl.ds(0, HALF)]
                remote(dst, dst, x2_send.at[0], x2_rest.at[block], to_x[0]).wait_recv()
            multiply(block_a, block_b)

        return carry

    lax.fori_loop(1, 11, step, 0)

    dot_in[head] = dot_mine[...]
    for device in (facing, facing_sibling, sibling):
        remote(dot_mine, dot_in.at[head], dot_send.at[0], dot_recv.at[head], device).start()

    for j in range(NYH):
        stays = jnp.logical_and(yh == j, y_core == core)

        @pl.when(jnp.logical_not(stays))
        def _(j=j):
            remote(
                y_send, y_land.at[y_half, core], y_ssem.at[j], y_rsem.at[y_half, core],
                at(j, z, x, ylo, y_core),
            ).wait_send()

    for copy in give:
        copy.wait_send()

    def sent(ref, sem):
        remote(ref, ref, sem.at[0], dot_recv.at[0], facing).wait_send()

    sent(w1.at[0, pl.ds(0, 48)], x1_send)
    sent(w1.at[pl.ds(0, NZ - 1)], z1_send)
    sent(w2.at[pl.ds(0, NZ - 1), pl.ds(0, 16)], z2_send)
    sent(w2.at[:, pl.ds(0, 32)], x2_send)
    sent(w2.at[:, pl.ds(0, 16)], fwd_send)

    for k in range(1, 4):
        other = (head + k) % 4
        remote(dot_mine, dot_in.at[other], dot_send.at[0], dot_recv.at[other], sibling).wait_recv()
    dots = dot_in[0] + dot_in[1] + dot_in[2] + dot_in[3]
    row_dot = jnp.sum(dots, axis=0, keepdims=True) / QR
    row_dot = jnp.broadcast_to(row_dot, (128, TOK)).T[:, 0:1]

    def arrived(block, carry):
        remote(
            part_in.at[block], part_in.at[block], part_send.at[0], part_recv.at[block], facing
        ).wait_recv()
        return carry

    lax.fori_loop(0, NZ, arrived, 0)
    whole = part[ylo] + part_in[...]
    d_normed = whole[:, 0:24, :].reshape(SHARE, TOK).T
    d_latent[...] = whole[:, 24:32, :].reshape(LSHARE, TOK).T.astype(jnp.bfloat16)
    columns = pl.ds(pl.multiple_of(head * SHARE, 128), SHARE)
    root_mean = root[:, 0:1]
    normed = q_lat[:, columns].astype(jnp.float32) / root_mean
    scaled = gain[:, columns] * d_normed
    d_query[...] = ((scaled - normed * row_dot) / root_mean).astype(jnp.bfloat16)
    sent(part_in, part_send)
    sent(dot_in.at[pl.ds(0, 3)], dot_send)


def on_device(q_cot, k_cot, q_latent, q_gain, w_uq, w_uk):
    vmem = pl.BlockSpec(memory_space=pltpu.VMEM)
    hbm = pl.BlockSpec(memory_space=pl.ANY)
    f32, bf16 = jnp.float32, jnp.bfloat16
    dma = pltpu.SemaphoreType.DMA
    return pl.pallas_call(
        kernel,
        out_shape=(
            jax.ShapeDtypeStruct((TOK, SHARE), bf16),
            jax.ShapeDtypeStruct((TOK, LSHARE), bf16),
        ),
        in_specs=[hbm, hbm, hbm, vmem, vmem, vmem],
        out_specs=(vmem, vmem),
        scratch_shapes=[
            pltpu.VMEM((2, 2, TOK, 256), bf16),
            pltpu.VMEM((2, 2, 2 * TOK, 512), bf16),
            pltpu.VMEM((NZ, 64, C1), bf16),
            pltpu.VMEM((NZ, 64, C2), bf16),
            pltpu.VMEM((2, 2, 16, 768), bf16),
            pltpu.VMEM((16, 768), bf16),
            pltpu.VMEM((16, 768), f32),
            pltpu.VMEM((16, 2048), f32),
            pltpu.VMEM((TOK, QR), bf16),
            pltpu.VMEM((TOK, 128), f32),
            pltpu.VMEM((2, SHARE, TOK), f32),
            pltpu.VMEM((128, 5 * TOK), f32),
            pltpu.VMEM((2, NZ, 32, TOK), f32),
            pltpu.VMEM((NZ, 32, TOK), f32),
            pltpu.VMEM((8, TOK), f32),
            pltpu.VMEM((4, 8, TOK), f32),
            pltpu.VMEM((1, QR), f32),
            dma((7,)),
            dma((6,)),
            dma((6,)),
            dma((4,)),
            dma((2, 2)),
            dma((1,)),
            dma((NX,)),
            dma((1,)),
            dma((NZ, NX)),
            dma((1,)),
            dma((NZ,)),
            dma((1,)),
            dma((2, NZ)),
            dma((NZ,)),
            dma((1,)),
            dma((1,)),
            dma((NZ,)),
            dma((1,)),
            dma((4,)),
        ],
        compiler_params=pltpu.CompilerParams(
            collective_id=0, has_side_effects=True, vmem_limit_bytes=62 * 2**20
        ),
        name="latent_backward",
    )(q_cot, k_cot, q_latent, q_gain, w_uq, w_uk)


def solution(mesh):
    return jax.shard_map(
        on_device,
        mesh=mesh,
        in_specs=(
            P("dp", "head"),
            P("dp", "head"),
            P("dp", None),
            P(),
            P("dp", "head"),
            P("dp", "head"),
        ),
        out_specs=(P("dp", "head"), P("dp", "head")),
        check_vma=False,
    )
```

```python
import jax
import jax.numpy as jnp
from jax import lax
from jax.experimental import pallas as pl
from jax.experimental.pallas import tpu as pltpu
from jax.sharding import PartitionSpec as P

norm_eps = 1e-06
MESH = pl.DeviceIdType.MESH

NX, NZ, NYH = 4, 16, 4
TOK, QR, KVR = 256, 1536, 512
QF, KF = 1536, 1024
C1 = 1024
C2 = 1792
HALF = C2 // 2
SHARE = QR // 4
LSHARE = KVR // 4


def kernel(
    q_cot, k_cot, q_lat_hbm, gain_flat, w_uq, w_uk, d_query, d_latent,
    a1, a2, w1, w2, y_land, y_send, stage1, stage2, q_lat, root, gain_normed, products,
    part, part_in, dot_mine, dot_in, gain,
    local_sem, a_send, a_recv, y_ssem, y_rsem, x1_send, x1_recv,
    z1_send, z1_recv, z2_send, z2_recv, x2_send, x2_first, x2_rest, fwd_send,
    part_send, part_recv, dot_send, dot_recv,
):
    dp, head = lax.axis_index("dp"), lax.axis_index("head")
    x, z, yh = dp % NX, (dp // NX) % NZ, dp // (NX * NZ)
    ylo, core = head // 2, head % 2

    def at(nyh, nz, nx, nylo, ncore):
        return ((nyh * NZ + nz) * NX + nx, nylo * 2 + ncore)

    xr, xl, xo = (x + 1) % NX, (x + NX - 1) % NX, (x + 2) % NX
    zr, zl = (z + 1) % NZ, (z + NZ - 1) % NZ
    sibling = at(yh, z, x, ylo, 1 - core)
    facing = at(yh, z, x, 1 - ylo, core)
    facing_sibling = at(yh, z, x, 1 - ylo, 1 - core)
    to_x = (at(yh, z, xr, ylo, core), at(yh, z, xl, ylo, core))
    to_x_over = at(yh, z, xo, ylo, core)
    to_z = (at(yh, zr, x, ylo, core), at(yh, zl, x, ylo, core))

    def remote(src, dst, ssem, rsem, device):
        return pltpu.make_async_remote_copy(
            src_ref=src, dst_ref=dst, send_sem=ssem, recv_sem=rsem,
            device_id=device, device_id_type=MESH,
        )

    def cotangents():
        for h in range(2):
            yield q_cot.at[:, pl.ds(h * 768, 512)], a2.at[core, h, pl.ds(0, TOK)]
            yield q_cot.at[:, pl.ds(h * 768 + 512, 256)], a1.at[core, h]
            yield k_cot.at[:, pl.ds(h * 512, 512)], a2.at[core, h, pl.ds(TOK, TOK)]

    own_lat = pltpu.make_async_copy(q_lat_hbm, q_lat, local_sem.at[6])
    own_lat.start()
    own_rows = [
        pltpu.make_async_copy(src, dst, local_sem.at[i])
        for i, (src, dst) in enumerate(cotangents())
    ]
    for copy in own_rows:
        copy.start()

    barrier = pltpu.get_barrier_semaphore()
    partners = [to_x[0], to_x[1], to_x_over, to_z[0], to_z[1], facing, facing_sibling, sibling]
    for j in range(1, NYH):
        for c in range(2):
            partners.append(at((yh + j) % NYH, z, x, ylo, c))
    for device in partners:
        pl.semaphore_signal(barrier, inc=1, device_id=device, device_id_type=MESH)

    uq = w_uq[...].astype(jnp.float32)
    uk = w_uk[...].astype(jnp.float32)
    for h in range(2):
        stage1[8 * h : 8 * h + 6] = uq[:, h * 768 : (h + 1) * 768]
        stage1[8 * h + 6 : 8 * h + 8, 0:512] = uk[:, h * 512 : (h + 1) * 512]
        stage1[8 * h + 6 : 8 * h + 8, 512:768] = jnp.zeros((2, 256), jnp.float32)
    y_send[...] = stage1[...].astype(jnp.bfloat16)

    pl.semaphore_wait(barrier, len(partners))

    y_core, y_half = yh % 2, yh // 2
    for j in range(NYH):
        stays = jnp.logical_and(yh == j, y_core == core)

        @pl.when(jnp.logical_not(stays))
        def _(j=j):
            remote(
                y_send, y_land.at[y_half, core], y_ssem.at[j], y_rsem.at[y_half, core],
                at(j, z, x, ylo, y_core),
            ).start()

    mine = y_core == core

    @pl.when(mine)
    def _():
        y_land[y_half, core] = y_send[...]

    give = [
        remote(src, dst, a_send.at[i], a_recv.at[i], sibling)
        for i, (src, dst) in enumerate(cotangents())
    ]
    for copy in give:
        copy.start()

    gain[...] = gain_flat[...].reshape(1, QR)
    own_lat.wait()
    latent = q_lat[...].astype(jnp.float32)
    root_mean = jnp.sqrt(jnp.mean(latent * latent, axis=1, keepdims=True) + norm_eps)
    root[...] = jnp.broadcast_to(root_mean, (TOK, 128))
    for half in range(2):
        columns = pl.ds(pl.multiple_of((core + 2 * half) * SHARE, 128), SHARE)
        normed = q_lat[:, columns].astype(jnp.float32) / root_mean
        gain_normed[half] = (gain[:, columns] * normed).T
    dot_mine[...] = jnp.zeros_like(dot_mine)

    for half in range(2):
        for c in range(2):
            source_yh = core + 2 * half
            local = jnp.logical_and(source_yh == yh, core == c)

            @pl.when(jnp.logical_not(local))
            def _(half=half, c=c, source_yh=source_yh):
                remote(
                    y_send, y_land.at[half, c], y_ssem.at[0], y_rsem.at[half, c],
                    at((yh + 1) % NYH, z, x, ylo, c),
                ).wait_recv()

            piece = y_land[half, c].astype(jnp.float32)
            for h in range(2):
                rank, latents, group = piece[8 * h : 8 * h + 6], piece[8 * h + 6 : 8 * h + 8], 2 * c + h
                stage2[6 * half : 6 * half + 6, group * 512 : group * 512 + 512] = rank[:, 0:512]
                stage2[12 + 2 * half : 14 + 2 * half, group * 512 : group * 512 + 512] = latents[:, 0:512]
                if group < 3:
                    stage1[6 * half : 6 * half + 6, group * 256 : group * 256 + 256] = rank[:, 512:768]
                elif half == 0:
                    stage1[12:16, 0:256] = rank[0:4, 512:768]
                    stage1[12:14, 256:512] = rank[4:6, 512:768]
                else:
                    stage1[14:16, 256:512] = rank[0:2, 512:768]
                    stage1[12:16, 512:768] = rank[2:6, 512:768]

    def rows_of(nx):
        return pl.ds(pl.multiple_of(nx * 16, 16), 16)

    w1[z, rows_of(x), 0:768] = stage1[...].astype(jnp.bfloat16)
    w1[z, rows_of(x), 768:C1] = stage2[:, C2:2048].astype(jnp.bfloat16)
    w2[z, rows_of(x), :] = stage2[:, 0:C2].astype(jnp.bfloat16)

    def ring2(way, block):
        src = w2.at[block, rows_of(x)]
        return remote(src, src, z2_send.at[0], z2_recv.at[block], to_z[way])

    def ring2_half(way, block):
        src = w2.at[block, rows_of(x), pl.ds(way * HALF, HALF)]
        return remote(src, src, z2_send.at[0], z2_recv.at[block], to_z[way])

    def cross(way, block, half, first):
        src = w2.at[block, rows_of(x), pl.ds(half * HALF, HALF)]
        sem = x2_first.at[way, block] if first else x2_rest.at[block]
        return remote(src, src, x2_send.at[0], sem, to_x[way])

    def start_cross(block):
        for way in range(2):
            cross(way, block, way, True).start()
        for way in range(2):
            cross(way, block, 1 - way, False).start()

    def ring1(way, block, nx):
        src = w1.at[block, rows_of(nx)]
        return remote(src, src, z1_send.at[0], z1_recv.at[block, nx], to_z[way])

    ring2(0, z).start()
    ring2(1, z).start()
    src1 = w1.at[z, rows_of(x)]
    for k, device in enumerate((to_x[0], to_x[1], to_x_over)):
        remote(src1, src1, x1_send.at[0], x1_recv.at[x], device).start()
    ring1(0, z, x).start()
    ring1(1, z, x).start()
    start_cross(z)

    for nx in (xr, xl, xo):
        dst = w1.at[z, rows_of(nx)]
        remote(dst, dst, x1_send.at[0], x1_recv.at[nx], to_x_over).wait_recv()
        ring1(0, z, nx).start()
        ring1(1, z, nx).start()

    for i in range(6):
        own_rows[i].wait()
        give[i].wait_recv()

    def multiply(block_a, block_b, second):
        def both(ref, start, size):
            return jnp.concatenate(
                [ref[block_a, :, start : start + size], ref[block_b, :, start : start + size]], axis=0
            )

        def times(left, right):
            return lax.dot_general(
                left, right, (((1,), (1,)), ((), ())), preferred_element_type=jnp.float32
            )

        total = times(both(w2, 0, 512), a2[0, 0])
        for t in range(1, 3):
            total = total + times(both(w2, t * 512, 512), a2[t // 2, t % 2])
        last = jnp.concatenate([both(w2, 1536, 256), both(w1, 768, 256)], axis=1)
        total = total + times(last, a2[1, 1])
        products[:, 0 : 2 * TOK] = total
        firsts = [both(w1, t * 256, 256) for t in range(3)]
        total = times(firsts[0], a1[0, 0]) + times(firsts[1], a1[0, 1]) + times(firsts[2], a1[1, 0])
        products[:, 0:TOK] += total
        for t in range(3):
            products[:, (2 + t) * TOK : (3 + t) * TOK] = times(firsts[t], a1[1, 1])
        for base in range(0, 128, 16):
            for t in range(3):
                products[base + 4 * t : base + 4 * t + 4, 0:TOK] += products[
                    base + 12 : base + 16, (2 + t) * TOK : (3 + t) * TOK
                ]

        def give_out(g, block):
            for half in range(2):
                for nx in range(NX):
                    base = g * 64 + nx * 16
                    part[half, block, 6 * nx : 6 * nx + 6, :] = products[
                        base + 6 * half : base + 6 * half + 6, 0:TOK
                    ]
                    part[half, block, 24 + 2 * nx : 26 + 2 * nx, :] = products[
                        base + 12 + 2 * half : base + 14 + 2 * half, TOK : 2 * TOK
                    ]
            send_part(block).start()
            dot = dot_mine[...]
            for half in range(2):
                weighted = (
                    part[half, block, 0:24, :]
                    * gain_normed[half, pl.ds(pl.multiple_of(block * 24, 8), 24), :]
                )
                dot = dot + (weighted[0:8] + weighted[8:16] + weighted[16:24])
            dot_mine[...] = dot

        give_out(0, block_a)

        @pl.when(second)
        def _():
            give_out(1, block_b)

    def send_part(block):
        return remote(
            part.at[1 - ylo, block], part_in.at[block], part_send.at[0], part_recv.at[block], facing
        )

    def forward(block):
        for way, nx in ((0, xl), (1, xr)):
            src = w2.at[block, rows_of(nx), pl.ds(way * HALF, HALF)]
            remote(src, src, fwd_send.at[0], x2_first.at[way, block], to_x[way]).wait_recv()
            remote(src, src, fwd_send.at[0], x2_rest.at[block], to_x[way]).start()

    def ring1_unit(unit):
        step_at, k = unit // 4 + 1, unit % 4
        nx = jnp.where(k == 0, x, jnp.where(k == 1, xr, jnp.where(k == 2, xl, xo)))
        behind, ahead = (z - step_at + NZ) % NZ, (z + step_at) % NZ
        ring1(0, behind, nx).wait_recv()

        @pl.when(jnp.logical_or(step_at < 7, jnp.logical_and(step_at == 7, k < 2)))
        def _():
            ring1(0, behind, nx).start()

        @pl.when(step_at < 8)
        def _():
            ring1(1, ahead, nx).wait_recv()

        @pl.when(jnp.logical_or(step_at < 7, jnp.logical_and(step_at == 7, k >= 2)))
        def _():
            ring1(1, ahead, nx).start()

    def step(i, carry):
        behind, ahead = (z - i + NZ) % NZ, (z + i) % NZ

        @pl.when(i <= 8)
        def _():
            ring2(0, behind).wait_recv()

            @pl.when(i < 7)
            def _():
                ring2(0, behind).start()

            @pl.when(i == 7)
            def _():
                ring2_half(0, behind).start()

            start_cross(behind)

        @pl.when(i < 8)
        def _():
            ring2(1, ahead).wait_recv()

            @pl.when(i < 7)
            def _():
                ring2(1, ahead).start()

            @pl.when(i == 7)
            def _():
                ring2_half(1, ahead).start()

            start_cross(ahead)

        @pl.when(i <= 9)
        def _():
            forward((z - i + 1 + NZ) % NZ)

        @pl.when(jnp.logical_and(i >= 2, i <= 8))
        def _():
            forward((z + i - 1) % NZ)

        @pl.when(i <= 8)
        def _():
            for k in range(3):
                ring1_unit(3 * i - 3 + k)

        @pl.when(i >= 9)
        def _():
            for k in range(4):
                ring1_unit(4 * i - 12 + k)

        @pl.when(i >= 2)
        def _():
            d = i - 2
            block_a, block_b = (z - d + NZ) % NZ, (z + d) % NZ
            second = jnp.logical_and(d >= 1, d < 8)

            def rest(block):
                dst = w2.at[block, :, pl.ds(0, HALF)]
                remote(dst, dst, x2_send.at[0], x2_rest.at[block], to_x[0]).wait_recv()

            rest(block_a)

            @pl.when(second)
            def _():
                rest(block_b)

            multiply(block_a, block_b, second)

        return carry

    lax.fori_loop(1, 11, step, 0)

    dot_in[head] = dot_mine[...]
    for device in (facing, facing_sibling, sibling):
        remote(dot_mine, dot_in.at[head], dot_send.at[0], dot_recv.at[head], device).start()

    for j in range(NYH):
        stays = jnp.logical_and(yh == j, y_core == core)

        @pl.when(jnp.logical_not(stays))
        def _(j=j):
            remote(
                y_send, y_land.at[y_half, core], y_ssem.at[j], y_rsem.at[y_half, core],
                at(j, z, x, ylo, y_core),
            ).wait_send()

    for copy in give:
        copy.wait_send()

    def sent(ref, sem):
        remote(ref, ref, sem.at[0], dot_recv.at[0], facing).wait_send()

    sent(w1.at[0, pl.ds(0, 48)], x1_send)
    sent(w1.at[pl.ds(0, NZ - 1)], z1_send)
    sent(w2.at[pl.ds(0, NZ - 1), pl.ds(0, 16)], z2_send)
    sent(w2.at[:, pl.ds(0, 32)], x2_send)
    sent(w2.at[:, pl.ds(0, 16)], fwd_send)

    for k in range(1, 4):
        other = (head + k) % 4
        remote(dot_mine, dot_in.at[other], dot_send.at[0], dot_recv.at[other], sibling).wait_recv()
    dots = dot_in[0] + dot_in[1] + dot_in[2] + dot_in[3]
    row_dot = jnp.sum(dots, axis=0, keepdims=True) / QR
    row_dot = jnp.broadcast_to(row_dot, (128, TOK)).T[:, 0:1]

    def arrived(block, carry):
        remote(
            part_in.at[block], part_in.at[block], part_send.at[0], part_recv.at[block], facing
        ).wait_recv()
        return carry

    lax.fori_loop(0, NZ, arrived, 0)
    whole = part[ylo] + part_in[...]
    d_normed = whole[:, 0:24, :].reshape(SHARE, TOK).T
    d_latent[...] = whole[:, 24:32, :].reshape(LSHARE, TOK).T.astype(jnp.bfloat16)
    columns = pl.ds(pl.multiple_of(head * SHARE, 128), SHARE)
    root_mean = root[:, 0:1]
    normed = q_lat[:, columns].astype(jnp.float32) / root_mean
    scaled = gain[:, columns] * d_normed
    d_query[...] = ((scaled - normed * row_dot) / root_mean).astype(jnp.bfloat16)
    sent(part_in, part_send)
    sent(dot_in.at[pl.ds(0, 3)], dot_send)


def hand_over(query_in, latent_in, query_out, latent_out):
    query_out[...] = query_in[...]
    latent_out[...] = latent_in[...]


def on_device(q_cot, k_cot, q_latent, q_gain, w_uq, w_uk):
    vmem = pl.BlockSpec(memory_space=pltpu.VMEM)
    hbm = pl.BlockSpec(memory_space=pl.ANY)
    f32, bf16 = jnp.float32, jnp.bfloat16
    dma = pltpu.SemaphoreType.DMA
    out_shape = (
        jax.ShapeDtypeStruct((TOK, SHARE), bf16),
        jax.ShapeDtypeStruct((TOK, LSHARE), bf16),
    )
    results = pl.pallas_call(
        kernel,
        out_shape=out_shape,
        in_specs=[hbm, hbm, hbm, vmem, vmem, vmem],
        out_specs=(vmem, vmem),
        scratch_shapes=[
            pltpu.VMEM((2, 2, TOK, 256), bf16),
            pltpu.VMEM((2, 2, 2 * TOK, 512), bf16),
            pltpu.VMEM((NZ, 64, C1), bf16),
            pltpu.VMEM((NZ, 64, C2), bf16),
            pltpu.VMEM((2, 2, 16, 768), bf16),
            pltpu.VMEM((16, 768), bf16),
            pltpu.VMEM((16, 768), f32),
            pltpu.VMEM((16, 2048), f32),
            pltpu.VMEM((TOK, QR), bf16),
            pltpu.VMEM((TOK, 128), f32),
            pltpu.VMEM((2, SHARE, TOK), f32),
            pltpu.VMEM((128, 5 * TOK), f32),
            pltpu.VMEM((2, NZ, 32, TOK), f32),
            pltpu.VMEM((NZ, 32, TOK), f32),
            pltpu.VMEM((8, TOK), f32),
            pltpu.VMEM((4, 8, TOK), f32),
            pltpu.VMEM((1, QR), f32),
            dma((7,)),
            dma((6,)),
            dma((6,)),
            dma((4,)),
            dma((2, 2)),
            dma((1,)),
            dma((NX,)),
            dma((1,)),
            dma((NZ, NX)),
            dma((1,)),
            dma((NZ,)),
            dma((1,)),
            dma((2, NZ)),
            dma((NZ,)),
            dma((1,)),
            dma((1,)),
            dma((NZ,)),
            dma((1,)),
            dma((4,)),
        ],
        compiler_params=pltpu.CompilerParams(
            collective_id=0, has_side_effects=True, vmem_limit_bytes=62 * 2**20
        ),
        name="latent_backward",
    )(q_cot, k_cot, q_latent, q_gain, w_uq, w_uk)
    return pl.pallas_call(
        hand_over, out_shape=out_shape, in_specs=[vmem, vmem], out_specs=(vmem, vmem), name="hand_over"
    )(*results)


def solution(mesh):
    return jax.shard_map(
        on_device,
        mesh=mesh,
        in_specs=(
            P("dp", "head"),
            P("dp", "head"),
            P("dp", None),
            P(),
            P("dp", "head"),
            P("dp", "head"),
        ),
        out_specs=(P("dp", "head"), P("dp", "head")),
        check_vma=False,
    )
```

```python
import jax
import jax.numpy as jnp
from jax import lax
from jax.experimental import pallas as pl
from jax.experimental.pallas import tpu as pltpu
from jax.sharding import PartitionSpec as P

norm_eps = 1e-06
MESH = pl.DeviceIdType.MESH

NX, NZ, NYH = 4, 16, 4
TOK, QR, KVR = 256, 1536, 512
QF, KF = 1536, 1024
C1 = 1024
C2 = 1792
HALF = C2 // 2
SHARE = QR // 4
LSHARE = KVR // 4


def kernel(
    q_cot, k_cot, q_lat_hbm, gain_flat, w_uq, w_uk, d_query, d_latent,
    a1, a2, w1, w2, y_land, y_send, stage1, stage2, q_lat, root, gain_normed, products,
    part, part_in, dot_mine, dot_in, gain,
    local_sem, a_send, a_recv, y_ssem, y_rsem, x1_send, x1_recv,
    z1_send, z1_recv, z2_send, z2_recv, x2_send, x2_first, x2_rest, fwd_send,
    part_send, part_recv, dot_send, dot_recv,
):
    dp, head = lax.axis_index("dp"), lax.axis_index("head")
    x, z, yh = dp % NX, (dp // NX) % NZ, dp // (NX * NZ)
    ylo, core = head // 2, head % 2

    def at(nyh, nz, nx, nylo, ncore):
        return ((nyh * NZ + nz) * NX + nx, nylo * 2 + ncore)

    xr, xl, xo = (x + 1) % NX, (x + NX - 1) % NX, (x + 2) % NX
    zr, zl = (z + 1) % NZ, (z + NZ - 1) % NZ
    sibling = at(yh, z, x, ylo, 1 - core)
    facing = at(yh, z, x, 1 - ylo, core)
    facing_sibling = at(yh, z, x, 1 - ylo, 1 - core)
    to_x = (at(yh, z, xr, ylo, core), at(yh, z, xl, ylo, core))
    to_x_over = at(yh, z, xo, ylo, core)
    to_z = (at(yh, zr, x, ylo, core), at(yh, zl, x, ylo, core))

    def remote(src, dst, ssem, rsem, device):
        return pltpu.make_async_remote_copy(
            src_ref=src, dst_ref=dst, send_sem=ssem, recv_sem=rsem,
            device_id=device, device_id_type=MESH,
        )

    def cotangents():
        for h in range(2):
            yield q_cot.at[:, pl.ds(h * 768, 512)], a2.at[core, h, pl.ds(0, TOK)]
            yield q_cot.at[:, pl.ds(h * 768 + 512, 256)], a1.at[core, h]
            yield k_cot.at[:, pl.ds(h * 512, 512)], a2.at[core, h, pl.ds(TOK, TOK)]

    own_lat = pltpu.make_async_copy(q_lat_hbm, q_lat, local_sem.at[6])
    own_lat.start()
    own_rows = [
        pltpu.make_async_copy(src, dst, local_sem.at[i])
        for i, (src, dst) in enumerate(cotangents())
    ]
    for copy in own_rows:
        copy.start()

    barrier = pltpu.get_barrier_semaphore()
    partners = [to_x[0], to_x[1], to_x_over, to_z[0], to_z[1], facing, facing_sibling, sibling]
    for j in range(1, NYH):
        for c in range(2):
            partners.append(at((yh + j) % NYH, z, x, ylo, c))
    for device in partners:
        pl.semaphore_signal(barrier, inc=1, device_id=device, device_id_type=MESH)

    uq = w_uq[...].astype(jnp.float32)
    uk = w_uk[...].astype(jnp.float32)
    for h in range(2):
        stage1[8 * h : 8 * h + 6] = uq[:, h * 768 : (h + 1) * 768]
        stage1[8 * h + 6 : 8 * h + 8, 0:512] = uk[:, h * 512 : (h + 1) * 512]
        stage1[8 * h + 6 : 8 * h + 8, 512:768] = jnp.zeros((2, 256), jnp.float32)
    y_send[...] = stage1[...].astype(jnp.bfloat16)

    pl.semaphore_wait(barrier, len(partners))

    y_core, y_half = yh % 2, yh // 2
    for j in range(NYH):
        stays = jnp.logical_and(yh == j, y_core == core)

        @pl.when(jnp.logical_not(stays))
        def _(j=j):
            remote(
                y_send, y_land.at[y_half, core], y_ssem.at[j], y_rsem.at[y_half, core],
                at(j, z, x, ylo, y_core),
            ).start()

    mine = y_core == core

    @pl.when(mine)
    def _():
        y_land[y_half, core] = y_send[...]

    give = [
        remote(src, dst, a_send.at[i], a_recv.at[i], sibling)
        for i, (src, dst) in enumerate(cotangents())
    ]
    for copy in give:
        copy.start()

    gain[...] = gain_flat[...].reshape(1, QR)
    own_lat.wait()
    latent = q_lat[...].astype(jnp.float32)
    root_mean = jnp.sqrt(jnp.mean(latent * latent, axis=1, keepdims=True) + norm_eps)
    root[...] = jnp.broadcast_to(root_mean, (TOK, 128))
    for half in range(2):
        columns = pl.ds(pl.multiple_of((core + 2 * half) * SHARE, 128), SHARE)
        normed = q_lat[:, columns].astype(jnp.float32) / root_mean
        gain_normed[half] = (gain[:, columns] * normed).T
    dot_mine[...] = jnp.zeros_like(dot_mine)

    for half in range(2):
        for c in range(2):
            source_yh = core + 2 * half
            local = jnp.logical_and(source_yh == yh, core == c)

            @pl.when(jnp.logical_not(local))
            def _(half=half, c=c, source_yh=source_yh):
                remote(
                    y_send, y_land.at[half, c], y_ssem.at[0], y_rsem.at[half, c],
                    at((yh + 1) % NYH, z, x, ylo, c),
                ).wait_recv()

            piece = y_land[half, c].astype(jnp.float32)
            for h in range(2):
                rank, latents, group = piece[8 * h : 8 * h + 6], piece[8 * h + 6 : 8 * h + 8], 2 * c + h
                stage2[6 * half : 6 * half + 6, group * 512 : group * 512 + 512] = rank[:, 0:512]
                stage2[12 + 2 * half : 14 + 2 * half, group * 512 : group * 512 + 512] = latents[:, 0:512]
                if group < 3:
                    stage1[6 * half : 6 * half + 6, group * 256 : group * 256 + 256] = rank[:, 512:768]
                elif half == 0:
                    stage1[12:16, 0:256] = rank[0:4, 512:768]
                    stage1[12:14, 256:512] = rank[4:6, 512:768]
                else:
                    stage1[14:16, 256:512] = rank[0:2, 512:768]
                    stage1[12:16, 512:768] = rank[2:6, 512:768]

    def rows_of(nx):
        return pl.ds(pl.multiple_of(nx * 16, 16), 16)

    w1[z, rows_of(x), 0:768] = stage1[...].astype(jnp.bfloat16)
    w1[z, rows_of(x), 768:C1] = stage2[:, C2:2048].astype(jnp.bfloat16)
    w2[z, rows_of(x), :] = stage2[:, 0:C2].astype(jnp.bfloat16)

    def ring2(way, block):
        src = w2.at[block, rows_of(x)]
        return remote(src, src, z2_send.at[0], z2_recv.at[block], to_z[way])

    def ring2_half(way, block):
        src = w2.at[block, rows_of(x), pl.ds(way * HALF, HALF)]
        return remote(src, src, z2_send.at[0], z2_recv.at[block], to_z[way])

    def cross(way, block, half, first):
        src = w2.at[block, rows_of(x), pl.ds(half * HALF, HALF)]
        sem = x2_first.at[way, block] if first else x2_rest.at[block]
        return remote(src, src, x2_send.at[0], sem, to_x[way])

    def start_cross(block):
        for way in range(2):
            cross(way, block, way, True).start()
        for way in range(2):
            cross(way, block, 1 - way, False).start()

    def ring1(way, block, nx):
        src = w1.at[block, rows_of(nx)]
        return remote(src, src, z1_send.at[0], z1_recv.at[block, nx], to_z[way])

    ring2(0, z).start()
    ring2(1, z).start()
    src1 = w1.at[z, rows_of(x)]
    for k, device in enumerate((to_x[0], to_x[1], to_x_over)):
        remote(src1, src1, x1_send.at[0], x1_recv.at[x], device).start()
    ring1(0, z, x).start()
    ring1(1, z, x).start()
    start_cross(z)

    for nx in (xr, xl, xo):
        dst = w1.at[z, rows_of(nx)]
        remote(dst, dst, x1_send.at[0], x1_recv.at[nx], to_x_over).wait_recv()
        ring1(0, z, nx).start()
        ring1(1, z, nx).start()

    for i in range(6):
        own_rows[i].wait()
        give[i].wait_recv()

    def multiply(block_a, block_b, second):
        def both(ref, start, size):
            return jnp.concatenate(
                [ref[block_a, :, start : start + size], ref[block_b, :, start : start + size]], axis=0
            )

        def times(left, right):
            return lax.dot_general(
                left, right, (((1,), (1,)), ((), ())), preferred_element_type=jnp.float32
            )

        total = times(both(w2, 0, 512), a2[0, 0])
        for t in range(1, 3):
            total = total + times(both(w2, t * 512, 512), a2[t // 2, t % 2])
        last = jnp.concatenate([both(w2, 1536, 256), both(w1, 768, 256)], axis=1)
        total = total + times(last, a2[1, 1])
        products[:, 0 : 2 * TOK] = total
        firsts = [both(w1, t * 256, 256) for t in range(3)]
        total = times(firsts[0], a1[0, 0]) + times(firsts[1], a1[0, 1]) + times(firsts[2], a1[1, 0])
        products[:, 0:TOK] += total
        for t in range(3):
            products[:, (2 + t) * TOK : (3 + t) * TOK] = times(firsts[t], a1[1, 1])
        for base in range(0, 128, 16):
            for t in range(3):
                products[base + 4 * t : base + 4 * t + 4, 0:TOK] += products[
                    base + 12 : base + 16, (2 + t) * TOK : (3 + t) * TOK
                ]

        def give_out(g, block):
            for half in range(2):
                for nx in range(NX):
                    base = g * 64 + nx * 16
                    part[half, block, 6 * nx : 6 * nx + 6, :] = products[
                        base + 6 * half : base + 6 * half + 6, 0:TOK
                    ]
                    part[half, block, 24 + 2 * nx : 26 + 2 * nx, :] = products[
                        base + 12 + 2 * half : base + 14 + 2 * half, TOK : 2 * TOK
                    ]
            send_part(block).start()
            dot = dot_mine[...]
            for half in range(2):
                weighted = (
                    part[half, block, 0:24, :]
                    * gain_normed[half, pl.ds(pl.multiple_of(block * 24, 8), 24), :]
                )
                dot = dot + (weighted[0:8] + weighted[8:16] + weighted[16:24])
            dot_mine[...] = dot

        give_out(0, block_a)

        @pl.when(second)
        def _():
            give_out(1, block_b)

    def send_part(block):
        return remote(
            part.at[1 - ylo, block], part_in.at[block], part_send.at[0], part_recv.at[block], facing
        )

    def forward(block):
        for way, nx in ((0, xl), (1, xr)):
            src = w2.at[block, rows_of(nx), pl.ds(way * HALF, HALF)]
            remote(src, src, fwd_send.at[0], x2_first.at[way, block], to_x[way]).wait_recv()
            remote(src, src, fwd_send.at[0], x2_rest.at[block], to_x[way]).start()

    def ring1_unit(unit):
        step_at, k = unit // 4 + 1, unit % 4
        nx = jnp.where(k == 0, x, jnp.where(k == 1, xr, jnp.where(k == 2, xl, xo)))
        behind, ahead = (z - step_at + NZ) % NZ, (z + step_at) % NZ
        ring1(0, behind, nx).wait_recv()

        @pl.when(jnp.logical_or(step_at < 7, jnp.logical_and(step_at == 7, k < 2)))
        def _():
            ring1(0, behind, nx).start()

        @pl.when(step_at < 8)
        def _():
            ring1(1, ahead, nx).wait_recv()

        @pl.when(jnp.logical_or(step_at < 7, jnp.logical_and(step_at == 7, k >= 2)))
        def _():
            ring1(1, ahead, nx).start()

    def step(i, carry):
        behind, ahead = (z - i + NZ) % NZ, (z + i) % NZ

        @pl.when(i <= 8)
        def _():
            ring2(0, behind).wait_recv()

            @pl.when(i < 7)
            def _():
                ring2(0, behind).start()

            @pl.when(i == 7)
            def _():
                ring2_half(0, behind).start()

            start_cross(behind)

        @pl.when(i < 8)
        def _():
            ring2(1, ahead).wait_recv()

            @pl.when(i < 7)
            def _():
                ring2(1, ahead).start()

            @pl.when(i == 7)
            def _():
                ring2_half(1, ahead).start()

            start_cross(ahead)

        @pl.when(i <= 8)
        def _():
            for k in range(3):
                ring1_unit(3 * i - 3 + k)

        @pl.when(i >= 9)
        def _():
            for k in range(4):
                ring1_unit(4 * i - 12 + k)

        @pl.when(i <= 9)
        def _():
            forward((z - i + 1 + NZ) % NZ)

        @pl.when(jnp.logical_and(i >= 2, i <= 8))
        def _():
            forward((z + i - 1) % NZ)

        @pl.when(i >= 2)
        def _():
            d = i - 2
            block_a, block_b = (z - d + NZ) % NZ, (z + d) % NZ
            second = jnp.logical_and(d >= 1, d < 8)

            def rest(block):
                dst = w2.at[block, :, pl.ds(0, HALF)]
                remote(dst, dst, x2_send.at[0], x2_rest.at[block], to_x[0]).wait_recv()

            rest(block_a)

            @pl.when(second)
            def _():
                rest(block_b)

            multiply(block_a, block_b, second)

        return carry

    lax.fori_loop(1, 11, step, 0)

    dot_in[head] = dot_mine[...]
    for device in (facing, facing_sibling, sibling):
        remote(dot_mine, dot_in.at[head], dot_send.at[0], dot_recv.at[head], device).start()

    for j in range(NYH):
        stays = jnp.logical_and(yh == j, y_core == core)

        @pl.when(jnp.logical_not(stays))
        def _(j=j):
            remote(
                y_send, y_land.at[y_half, core], y_ssem.at[j], y_rsem.at[y_half, core],
                at(j, z, x, ylo, y_core),
            ).wait_send()

    for copy in give:
        copy.wait_send()

    def sent(ref, sem):
        remote(ref, ref, sem.at[0], dot_recv.at[0], facing).wait_send()

    sent(w1.at[0, pl.ds(0, 48)], x1_send)
    sent(w1.at[pl.ds(0, NZ - 1)], z1_send)
    sent(w2.at[pl.ds(0, NZ - 1), pl.ds(0, 16)], z2_send)
    sent(w2.at[:, pl.ds(0, 32)], x2_send)
    sent(w2.at[:, pl.ds(0, 16)], fwd_send)

    for k in range(1, 4):
        other = (head + k) % 4
        remote(dot_mine, dot_in.at[other], dot_send.at[0], dot_recv.at[other], sibling).wait_recv()
    dots = dot_in[0] + dot_in[1] + dot_in[2] + dot_in[3]
    row_dot = jnp.sum(dots, axis=0, keepdims=True) / QR
    row_dot = jnp.broadcast_to(row_dot, (128, TOK)).T[:, 0:1]

    def arrived(block, carry):
        remote(
            part_in.at[block], part_in.at[block], part_send.at[0], part_recv.at[block], facing
        ).wait_recv()
        return carry

    lax.fori_loop(0, NZ, arrived, 0)
    whole = part[ylo] + part_in[...]
    d_normed = whole[:, 0:24, :].reshape(SHARE, TOK).T
    d_latent[...] = whole[:, 24:32, :].reshape(LSHARE, TOK).T.astype(jnp.bfloat16)
    columns = pl.ds(pl.multiple_of(head * SHARE, 128), SHARE)
    root_mean = root[:, 0:1]
    normed = q_lat[:, columns].astype(jnp.float32) / root_mean
    scaled = gain[:, columns] * d_normed
    d_query[...] = ((scaled - normed * row_dot) / root_mean).astype(jnp.bfloat16)
    sent(part_in, part_send)
    sent(dot_in.at[pl.ds(0, 3)], dot_send)


def hand_over(query_in, latent_in, query_out, latent_out, query, latent, sem_in, sem_out):
    ways = ((query_in, query, query_out), (latent_in, latent, latent_out))
    arriving = [pltpu.make_async_copy(a, b, sem_in.at[i]) for i, (a, b, _) in enumerate(ways)]
    leaving = [pltpu.make_async_copy(b, c, sem_out.at[i]) for i, (_, b, c) in enumerate(ways)]
    for copy in arriving:
        copy.start()
    for copy, onward in zip(arriving, leaving):
        copy.wait()
        onward.start()
    for copy in leaving:
        copy.wait()


def on_device(q_cot, k_cot, q_latent, q_gain, w_uq, w_uk):
    vmem = pl.BlockSpec(memory_space=pltpu.VMEM)
    hbm = pl.BlockSpec(memory_space=pl.ANY)
    f32, bf16 = jnp.float32, jnp.bfloat16
    dma = pltpu.SemaphoreType.DMA
    out_shape = (
        jax.ShapeDtypeStruct((TOK, SHARE), bf16),
        jax.ShapeDtypeStruct((TOK, LSHARE), bf16),
    )
    results = pl.pallas_call(
        kernel,
        out_shape=out_shape,
        in_specs=[hbm, hbm, hbm, vmem, vmem, vmem],
        out_specs=(vmem, vmem),
        scratch_shapes=[
            pltpu.VMEM((2, 2, TOK, 256), bf16),
            pltpu.VMEM((2, 2, 2 * TOK, 512), bf16),
            pltpu.VMEM((NZ, 64, C1), bf16),
            pltpu.VMEM((NZ, 64, C2), bf16),
            pltpu.VMEM((2, 2, 16, 768), bf16),
            pltpu.VMEM((16, 768), bf16),
            pltpu.VMEM((16, 768), f32),
            pltpu.VMEM((16, 2048), f32),
            pltpu.VMEM((TOK, QR), bf16),
            pltpu.VMEM((TOK, 128), f32),
            pltpu.VMEM((2, SHARE, TOK), f32),
            pltpu.VMEM((128, 5 * TOK), f32),
            pltpu.VMEM((2, NZ, 32, TOK), f32),
            pltpu.VMEM((NZ, 32, TOK), f32),
            pltpu.VMEM((8, TOK), f32),
            pltpu.VMEM((4, 8, TOK), f32),
            pltpu.VMEM((1, QR), f32),
            dma((7,)),
            dma((6,)),
            dma((6,)),
            dma((4,)),
            dma((2, 2)),
            dma((1,)),
            dma((NX,)),
            dma((1,)),
            dma((NZ, NX)),
            dma((1,)),
            dma((NZ,)),
            dma((1,)),
            dma((2, NZ)),
            dma((NZ,)),
            dma((1,)),
            dma((1,)),
            dma((NZ,)),
            dma((1,)),
            dma((4,)),
        ],
        compiler_params=pltpu.CompilerParams(
            collective_id=0, has_side_effects=True, vmem_limit_bytes=62 * 2**20
        ),
        name="latent_backward",
    )(q_cot, k_cot, q_latent, q_gain, w_uq, w_uk)
    return pl.pallas_call(
        hand_over,
        out_shape=out_shape,
        in_specs=[hbm, hbm],
        out_specs=(hbm, hbm),
        scratch_shapes=[
            pltpu.VMEM((TOK, SHARE), bf16),
            pltpu.VMEM((TOK, LSHARE), bf16),
            dma((2,)),
            dma((2,)),
        ],
        name="hand_over",
    )(*results)


def solution(mesh):
    return jax.shard_map(
        on_device,
        mesh=mesh,
        in_specs=(
            P("dp", "head"),
            P("dp", "head"),
            P("dp", None),
            P(),
            P("dp", "head"),
            P("dp", "head"),
        ),
        out_specs=(P("dp", "head"), P("dp", "head")),
        check_vma=False,
    )
```
